256 devices in a mesh: sp: 32 (over z, x), dp: 8 (over y, core).
Axes of the slice: x: 4, y: 4, z: 8, core: 2. Of those that a mesh axis runs over, the one named last changes fastest.
Arguments:
- query_in: bfloat16 [32768, 4096], P(('dp', 'sp')), parts along dimension 0, may hold values from -4.5 to 4.5
- key_input: bfloat16 [32768, 512], P(('dp', 'sp')), parts along dimension 0, may hold values from -4.5 to 4.5
- value_input: bfloat16 [32768, 512], P(('dp', 'sp')), parts along dimension 0, may hold values from -6 to 6
- grad_out: bfloat16 [32768, 4096], P(('dp', 'sp')), parts along dimension 0, may hold values from -6 to 6
Outputs:
- query_grad: bfloat16 [32768, 4096], P(('dp', 'sp')), parts along dimension 0
- key_gradient: bfloat16 [32768, 512], P(('dp', 'sp')), parts along dimension 0
- value_gradient: bfloat16 [32768, 512], P(('dp', 'sp')), parts along dimension 0
The draws below stay inside these ranges and needn't reach their ends.
There are 8 independent parts, one for each index of `dp`. The reference program is written for one: setup_inputs(seed, part) draws one part's arguments, and reference() takes and returns one part's arrays. A program takes and returns all parts, laid end to end along the dimension named above; each array names one. Nothing has to cross between parts.
All inputs are finite; a program needn't handle non-finite values.
Results may differ from the reference program's by a relative error of at most 0.012.
Values may be sent and summed in bfloat16 or wider, within the bound.
No kernel may reach another device: no remote copies, remote signals or barrier semaphores. Data moves between devices by JAX's collectives and lax.ppermute only.
A program may use at most 192 MiB of HBM per device.

```python
import jax
import jax.numpy as jnp
from jax import lax

QUERY_HEADS = 32
KEY_HEADS = 4
HEAD_WIDTH = 128
SEQS = 1
TOKEN_COUNT = 4096
QUERY_PER_KEY = 8


def draw_query_in(key, part):
    key = jax.random.fold_in(key, 1)
    final_result = jnp.clip(jax.random.normal(key, (TOKEN_COUNT, QUERY_HEADS * HEAD_WIDTH), jnp.float32), -4.5, 4.5)
    return final_result.astype(jnp.bfloat16)


def draw_key_input(key, part):
    key = jax.random.fold_in(key, 2)
    final_result = jnp.clip(jax.random.normal(key, (TOKEN_COUNT, KEY_HEADS * HEAD_WIDTH), jnp.float32), -4.5, 4.5)
    return final_result.astype(jnp.bfloat16)


def shard_levels(key, shape, split, smallest, high):
    factor_of = 1.0
    for dim, blocks in split:
        heights = jax.random.uniform(jax.random.fold_in(jax.random.fold_in(key, 6), dim), (blocks,), jnp.float32, smallest / len(split), high / len(split))
        factor_of = factor_of * jnp.repeat(jnp.exp(heights), shape[dim] // blocks).reshape((-1,) + (1,) * (len(shape) - 1 - dim))
    return factor_of


def bell_draw(own_key, shape, spread, limit, cuts=(), held_as=jnp.bfloat16):
    entries = jax.random.normal(own_key, shape, jnp.float32) * spread
    if len(cuts) > 0:
        entries = shard_levels(own_key, shape, cuts, -0.22, 0.18) * entries
    return jnp.clip(entries, min=-limit, max=limit).astype(held_as)


def setup_inputs(seed: int = 0, part: int = 0) -> dict:
    streams_of = jax.random.split(jax.random.key(seed), 5)
    part_keys = jax.random.split(jax.random.fold_in(streams_of[4], part), 5)
    return {
        "query_in": draw_query_in(jax.random.fold_in(jax.random.fold_in(streams_of[4], part), 71), part),
        "key_input": draw_key_input(jax.random.fold_in(jax.random.fold_in(streams_of[4], part), 71), part),
        "value_input": bell_draw(part_keys[2], (TOKEN_COUNT, KEY_HEADS * HEAD_WIDTH), 1.0, 6.0, ((0, 32),)),
        "grad_out": bell_draw(part_keys[3], (TOKEN_COUNT, QUERY_HEADS * HEAD_WIDTH), 1.0, 6.0, ((0, 32),)),
    }


def reference(query_in, key_input, value_input, grad_out):
    score_scale = HEAD_WIDTH ** -0.5
    sequence_length = query_in.shape[0]
    span = sequence_length // SEQS
    queries = query_in.reshape(SEQS, span, QUERY_HEADS, HEAD_WIDTH).transpose(2, 0, 1, 3)
    grads = grad_out.reshape(SEQS, span, QUERY_HEADS, HEAD_WIDTH).transpose(2, 0, 1, 3)
    key_tensor = jnp.repeat(key_input.reshape(SEQS, span, KEY_HEADS, HEAD_WIDTH).transpose(2, 0, 1, 3), QUERY_PER_KEY, axis=0)
    value_tensor = jnp.repeat(value_input.reshape(SEQS, span, KEY_HEADS, HEAD_WIDTH).transpose(2, 0, 1, 3), QUERY_PER_KEY, axis=0)
    positions = jnp.arange(span, dtype=jnp.int32)
    causal = positions[None, :] <= positions[:, None]

    def one_sequence(q_head, g_head, k_head, v_head):
        scores = jnp.dot(q_head, k_head.T, preferred_element_type=jnp.float32) * score_scale
        scores = jnp.where(causal, scores, jnp.float32(-1e30))
        row_peak = jnp.max(scores, axis=-1, keepdims=True)
        expon = jnp.exp(scores - row_peak)
        weights = expon / jnp.sum(expon, axis=-1, keepdims=True)
        weights16 = weights.astype(jnp.bfloat16)
        output = jnp.dot(weights16, v_head, preferred_element_type=jnp.float32)
        row_delta = jnp.sum(g_head.astype(jnp.float32) * output, axis=-1, keepdims=True)
        dweights = jnp.dot(g_head, v_head.T, preferred_element_type=jnp.float32)
        dscores = (weights * (dweights - row_delta)).astype(jnp.bfloat16)
        dquery = jnp.dot(dscores, k_head, preferred_element_type=jnp.float32) * score_scale
        key_delta = jnp.dot(dscores.T, q_head, preferred_element_type=jnp.float32) * score_scale
        value_delta = jnp.dot(weights16.T, g_head, preferred_element_type=jnp.float32)
        return dquery, key_delta, value_delta

    def one_head(items):
        q_head, g_head, k_head, v_head = items
        return lax.map(lambda inner: one_sequence(*inner), (q_head, g_head, k_head, v_head))

    dquery, key_delta, value_delta = lax.map(one_head, (queries, grads, key_tensor, value_tensor))
    query_grad = dquery.transpose(1, 2, 0, 3).reshape(sequence_length, QUERY_HEADS * HEAD_WIDTH).astype(jnp.bfloat16)
    key_gradient = key_delta.reshape(KEY_HEADS, QUERY_PER_KEY, SEQS, span, HEAD_WIDTH).sum(axis=1).transpose(1, 2, 0, 3)
    value_gradient = value_delta.reshape(KEY_HEADS, QUERY_PER_KEY, SEQS, span, HEAD_WIDTH).sum(axis=1).transpose(1, 2, 0, 3)
    key_gradient = key_gradient.reshape(sequence_length, KEY_HEADS * HEAD_WIDTH).astype(jnp.bfloat16)
    value_gradient = value_gradient.reshape(sequence_length, KEY_HEADS * HEAD_WIDTH).astype(jnp.bfloat16)
    return (query_grad, key_gradient, value_gradient)
```

```python
import jax
import jax.numpy as jnp
from jax import lax
from jax.experimental import pallas as pl
from jax.experimental.pallas import tpu as pltpu
from jax.sharding import Mesh, PartitionSpec as P

f32 = jnp.float32
bf16 = jnp.bfloat16
HEADS = 32
KEY_HEADS = 4
GROUP = HEADS // KEY_HEADS
W = 128
X, Z = 4, 8
SCALE = W ** -0.5
EXP2_SCALE = W ** -0.5 * 1.4426950408889634


def nt(a, b):
    return lax.dot_general(a, b, (((1,), (1,)), ((), ())), preferred_element_type=f32)


def nn(a, b):
    return lax.dot_general(a, b, (((1,), (0,)), ((), ())), preferred_element_type=f32)


def attention_kernel(z_ref, q_ref, g_ref, k_ref, v_ref, dq_ref, dk_ref, dv_ref, kt, ps, dps, ms, dka, dva):
    R = q_ref.shape[0]
    T = R
    nb = k_ref.shape[0] // T
    h = pl.program_id(0)
    z = z_ref[0]

    @pl.when(h == 0)
    def _():
        dka[...] = jnp.zeros_like(dka)
        dva[...] = jnp.zeros_like(dva)
        for j in range(nb):
            kt[:, j * T:(j + 1) * T] = k_ref[j * T:(j + 1) * T, :].T

    q = q_ref[...]
    g = g_ref[...]

    def tile(j, carry, diag):
        m, l, d = carry
        off = pl.multiple_of(j * T, T)
        s = nt(k_ref[pl.ds(off, T), :], q)
        dp = nt(v_ref[pl.ds(off, T), :], g)
        if diag:
            kpos = lax.broadcasted_iota(jnp.int32, (T, R), 0)
            qpos = lax.broadcasted_iota(jnp.int32, (T, R), 1)
            s = jnp.where(kpos <= qpos, s, -1e30)
        mj = jnp.max(s, axis=0, keepdims=True)
        mn = mj if diag else jnp.maximum(m, mj)
        p = jnp.exp2((s - mn) * EXP2_SCALE)
        ps[j] = p.astype(bf16)
        dps[j] = dp
        ms[j] = jnp.broadcast_to(mn, (8, R))
        lj = jnp.sum(p, axis=0, keepdims=True)
        dj = jnp.sum(p * dp, axis=0, keepdims=True)
        if diag:
            return mn, lj, dj
        a = jnp.exp2((m - mn) * EXP2_SCALE)
        return mn, l * a + lj, d * a + dj

    carry = tile(z, (None, None, None), True)
    m, l, d = lax.fori_loop(0, z, lambda j, cr: tile(j, cr, False), carry)
    rl = 1.0 / l
    delta = d * rl

    def back(j, dqt):
        off = pl.multiple_of(j * T, T)
        f = jnp.exp2((ms[j][0:1] - m) * EXP2_SCALE) * rl
        w = ps[j].astype(f32) * f
        ds = (w * (dps[j] - delta)).astype(bf16)
        dva[pl.ds(off, T), :] += nn(w.astype(bf16), g)
        dka[pl.ds(off, T), :] += nn(ds, q)
        return dqt + nn(kt[:, pl.ds(off, T)], ds)

    dqt = lax.fori_loop(0, z + 1, back, jnp.zeros((W, R), f32))
    dq_ref[...] = (dqt.T * SCALE).astype(bf16)

    @pl.when(h == GROUP - 1)
    def _():
        dk_ref[...] = (dka[...] * SCALE).astype(bf16)
        dv_ref[...] = dva[...].astype(bf16)


def attention(zi, q, g, k, v):
    R, N = q.shape[0], k.shape[0]
    nb = N // R
    full = pl.BlockSpec((N, W), lambda h, z: (0, 0))
    col = pl.BlockSpec((R, W), lambda h, z: (0, h))
    return pl.pallas_call(
        attention_kernel,
        grid_spec=pltpu.PrefetchScalarGridSpec(
            num_scalar_prefetch=1,
            grid=(GROUP,),
            in_specs=[col, col, full, full],
            out_specs=[col, full, full],
            scratch_shapes=[
                pltpu.VMEM((W, N), bf16),
                pltpu.VMEM((nb, R, R), bf16),
                pltpu.VMEM((nb, R, R), f32),
                pltpu.VMEM((nb, 8, R), f32),
                pltpu.VMEM((N, W), f32),
                pltpu.VMEM((N, W), f32),
            ],
        ),
        out_shape=[
            jax.ShapeDtypeStruct((R, GROUP * W), bf16),
            jax.ShapeDtypeStruct((N, W), bf16),
            jax.ShapeDtypeStruct((N, W), bf16),
        ],
        compiler_params=pltpu.CompilerParams(vmem_limit_bytes=48 * 2**20, dimension_semantics=("arbitrary",)),
    )(zi, q, g, k, v)


def local(query_in, key_input, value_input, grad_out):
    rows = query_in.shape[0]
    kv = jnp.concatenate(
        [key_input.reshape(rows, KEY_HEADS, W), value_input.reshape(rows, KEY_HEADS, W)], axis=2
    )
    kv = lax.all_to_all(kv, "x", split_axis=1, concat_axis=0, tiled=True).reshape(X * rows, 2 * W)
    kv_all = lax.all_gather(kv, "z", axis=0, tiled=True)
    q = lax.all_to_all(query_in.reshape(rows, X, GROUP * W), "x", 1, 0, tiled=True).reshape(X * rows, GROUP * W)
    g = lax.all_to_all(grad_out.reshape(rows, X, GROUP * W), "x", 1, 0, tiled=True).reshape(X * rows, GROUP * W)
    zi = lax.axis_index("z").astype(jnp.int32).reshape(1)
    dq, dk, dv = attention(zi, q, g, kv_all[:, :W], kv_all[:, W:])
    dq = lax.all_to_all(dq.reshape(X * rows, 1, GROUP * W), "x", 0, 1, tiled=True).reshape(rows, HEADS * W)
    dkv = lax.psum_scatter(jnp.concatenate([dk, dv], axis=1), "z", scatter_dimension=0, tiled=True)
    dkv = lax.all_to_all(dkv.reshape(X * rows, 1, 2 * W), "x", 0, 1, tiled=True)
    dk = dkv[:, :, :W].reshape(rows, KEY_HEADS * W)
    dv = dkv[:, :, W:].reshape(rows, KEY_HEADS * W)
    return dq, dk, dv


def solution(mesh):
    grid = Mesh(mesh.devices.reshape(Z, X, mesh.shape["dp"]), ("z", "x", "dp"))
    spec = P(("dp", "z", "x"), None)
    return jax.shard_map(local, mesh=grid, in_specs=(spec,) * 4, out_specs=(spec,) * 3, check_vma=False)
```

```python
import jax
import jax.numpy as jnp
from jax import lax
from jax.experimental import pallas as pl
from jax.experimental.pallas import tpu as pltpu
from jax.sharding import Mesh, PartitionSpec as P

f32 = jnp.float32
bf16 = jnp.bfloat16
HEADS = 32
KEY_HEADS = 4
GROUP = HEADS // KEY_HEADS
W = 128
X, Z = 4, 8
SCALE = W ** -0.5
EXP2_SCALE = W ** -0.5 * 1.4426950408889634
LIMIT = (80.0 / EXP2_SCALE) ** 2


def nt(a, b):
    return lax.dot_general(a, b, (((1,), (1,)), ((), ())), preferred_element_type=f32)


def nn(a, b):
    return lax.dot_general(a, b, (((1,), (0,)), ((), ())), preferred_element_type=f32)


def attention_kernel(z_ref, qg_ref, b0, b1, b2, b3, k4, v4, b5, b6, b7, dq_ref,
                     o0, o1, o2, ok3, ov3, ok4, ov4, ok5, ov5, o6, o7,
                     kr, vr, kt, ps, dps, dka, dva, shift, inv, delta, qn, gn, big):
    R = qg_ref.shape[0]
    T = 2 * R
    h = pl.program_id(0)
    z = z_ref[0]
    blocks = z + 1
    pairs = blocks // 2
    odd = (blocks % 2 == 1) & (pairs >= 1)

    def head(i, base):
        return qg_ref[:, pl.ds(pl.multiple_of(base + i * W, W), W)]

    @pl.when(h == 0)
    def _():
        dka[...] = jnp.zeros_like(dka)
        dva[...] = jnp.zeros_like(dva)
        for r, blk in enumerate((b0, b1, b2, b3, None, b5, b6, b7)):
            kb = k4[...] if blk is None else blk[:, :W]
            vb = v4[...] if blk is None else blk[:, W:]
            kr[r * R:(r + 1) * R, :] = kb
            vr[r * R:(r + 1) * R, :] = vb
            kt[:, r * R:(r + 1) * R] = kb.T
        kk = kr[...].astype(f32)
        kn = jnp.max(nt(jnp.ones((8, W), bf16), (kk * kk).astype(bf16)))
        qq = qg_ref[:, :GROUP * W].astype(f32)
        col = lax.broadcasted_iota(jnp.int32, (GROUP, GROUP * W), 1) // W
        own = lax.broadcasted_iota(jnp.int32, (GROUP, GROUP * W), 0)
        qnorm = jnp.max(nt((col == own).astype(bf16), (qq * qq).astype(bf16)))
        big[0] = kn * qnorm

    def forward_begin():
        shift[...] = jnp.zeros_like(shift)

        @pl.when(jnp.logical_not(big[0] <= LIMIT))
        def _():
            q = head(h, 0)

            def peak(r, m):
                s = nt(kr[pl.ds(pl.multiple_of(r * R, R), R), :], q)
                kpos = lax.broadcasted_iota(jnp.int32, (R, R), 0)
                qpos = lax.broadcasted_iota(jnp.int32, (R, R), 1)
                s = jnp.where((kpos <= qpos) | (r > 0), s, -1e30)
                return jnp.maximum(m, jnp.max(s, axis=0, keepdims=True))

            m = lax.fori_loop(0, blocks, peak, jnp.full((1, R), -1e30, f32))
            shift[...] = jnp.broadcast_to(m * EXP2_SCALE, shift.shape)

    def forward(t, carry, first, n, buf):
        l8, d8 = carry
        q, g = head(h, 0), head(h, GROUP * W)
        m = shift[0:1, :]
        for r in range(n):
            rows = pl.ds(r * R, R) if first else pl.ds(pl.multiple_of(t * T + r * R, R), R)
            s = nt(kr[rows, :], q)
            dp = nt(vr[rows, :], g)
            if first and r == 0:
                kpos = lax.broadcasted_iota(jnp.int32, (R, R), 0)
                qpos = lax.broadcasted_iota(jnp.int32, (R, R), 1)
                s = jnp.where(kpos <= qpos, s, -1e30)
            elif first:
                s = jnp.where(z >= r, s, -1e30)
            p = jnp.exp2(s * EXP2_SCALE - m)
            ps[buf, rows, :] = p.astype(bf16)
            dps[buf, rows, :] = dp
            l8 = l8 + p.reshape(R // 8, 8, R).sum(0)
            d8 = d8 + (p * dp).reshape(R // 8, 8, R).sum(0)
        return l8, d8

    def forward_end(carry):
        l = jnp.sum(carry[0], axis=0, keepdims=True)
        rl = 1.0 / l
        inv[...] = jnp.broadcast_to(rl, inv.shape)
        delta[...] = jnp.broadcast_to(jnp.sum(carry[1], axis=0, keepdims=True) * rl, delta.shape)
        rc = inv[...].T[:, 0:1]
        qn[...] = (head(h, 0).astype(f32) * rc).astype(bf16)
        gn[...] = (head(h, GROUP * W).astype(f32) * rc).astype(bf16)

    def back(t, dqt, n, buf, q, g, dl):
        for r in range(n):
            rows = pl.ds(pl.multiple_of(t * T + r * R, R), R)
            p = ps[buf, rows, :]
            ds = (p.astype(f32) * (dps[buf, rows, :] - dl)).astype(bf16)
            dva[rows, :] += nn(p, g)
            dka[rows, :] += nn(ds, q)
            dqt = dqt + nn(kt[:, rows], ds)
        return dqt

    zero = (jnp.zeros((8, R), f32), jnp.zeros((8, R), f32))
    zq = jnp.zeros((W, R), f32)

    @pl.when(h == 0)
    def _():
        forward_begin()
        c = forward(0, zero, True, 2, 0)
        c = lax.fori_loop(1, pairs, lambda t, c: forward(t, c, False, 2, 0), c)
        c = lax.cond(odd, lambda c: forward(pairs, c, False, 1, 0), lambda c: c, c)
        forward_end(c)

    @pl.when((h > 0) & (h < GROUP))
    def _():
        new, old = lax.rem(h, 2), lax.rem(h + 1, 2)
        q, g, dl = qn[...], gn[...], delta[0:1, :]
        rl = inv[0:1, :] * SCALE
        forward_begin()

        def both(t, c, first, n):
            f = forward(t, c[:2], first, n, new)
            return f + (back(t, c[2], n, old, q, g, dl),)

        c = both(0, zero + (zq,), True, 2)
        c = lax.fori_loop(1, pairs, lambda t, c: both(t, c, False, 2), c)
        c = lax.cond(odd, lambda c: both(pairs, c, False, 1), lambda c: c, c)
        dq_ref[...] = (c[2] * rl).T.astype(bf16)
        forward_end(c[:2])

    @pl.when(h == GROUP)
    def _():
        old = (GROUP - 1) % 2
        q, g, dl = qn[...], gn[...], delta[0:1, :]
        c = lax.fori_loop(0, jnp.maximum(pairs, 1), lambda t, c: back(t, c, 2, old, q, g, dl), zq)
        c = lax.cond(odd, lambda c: back(pairs, c, 1, old, q, g, dl), lambda c: c, c)
        dq_ref[...] = (c * (inv[0:1, :] * SCALE)).T.astype(bf16)
        for r, out in enumerate((o0, o1, o2, (ok3, ov3), (ok4, ov4), (ok5, ov5), o6, o7)):
            rows = slice(r * R, (r + 1) * R)
            dk = (dka[rows, :] * SCALE).astype(bf16)
            dv = dva[rows, :].astype(bf16)
            if isinstance(out, tuple):
                out[0][...] = dk
                out[1][...] = dv
            else:
                out[:, :W] = dk
                out[:, W:] = dv


def attention(zi, qg, blocks):
    R = qg.shape[0]
    N = Z * R
    wide, half = (R, 2 * W), (R, W)
    outs = [wide] * 3 + [half] * 6 + [wide] * 2

    def whole(shapes):
        return [pl.BlockSpec(s, lambda h, z: (0, 0)) for s in shapes]

    return pl.pallas_call(
        attention_kernel,
        grid_spec=pltpu.PrefetchScalarGridSpec(
            num_scalar_prefetch=1,
            grid=(GROUP + 1,),
            in_specs=whole([qg.shape] + [b.shape for b in blocks]),
            out_specs=[pl.BlockSpec((R, W), lambda h, z: (0, jnp.maximum(h, 1) - 1))] + whole(outs),
            scratch_shapes=[
                pltpu.VMEM((N, W), bf16),
                pltpu.VMEM((N, W), bf16),
                pltpu.VMEM((W, N), bf16),
                pltpu.VMEM((2, N, R), bf16),
                pltpu.VMEM((2, N, R), f32),
                pltpu.VMEM((N, W), f32),
                pltpu.VMEM((N, W), f32),
                pltpu.VMEM((8, R), f32),
                pltpu.VMEM((8, R), f32),
                pltpu.VMEM((8, R), f32),
                pltpu.VMEM((R, W), bf16),
                pltpu.VMEM((R, W), bf16),
                pltpu.SMEM((1,), f32),
            ],
        ),
        out_shape=[jax.ShapeDtypeStruct((R, GROUP * W), bf16)]
        + [jax.ShapeDtypeStruct(s, bf16) for s in outs],
        compiler_params=pltpu.CompilerParams(vmem_limit_bytes=60 * 2**20, dimension_semantics=("arbitrary",)),
    )(zi, qg, *blocks)


def up(v):
    return lax.ppermute(v, "z", [(i, (i + 1) % Z) for i in range(Z)])


def down(v):
    return lax.ppermute(v, "z", [(i, (i - 1) % Z) for i in range(Z)])


def add(a, b):
    return (a.astype(f32) + b.astype(f32)).astype(bf16)


def swap(v):
    return lax.all_to_all(v, "x", split_axis=0, concat_axis=0, tiled=True)


def local(query_in, key_input, value_input, grad_out):
    rows = query_in.shape[0]
    kv = jnp.concatenate(
        [key_input.reshape(rows, KEY_HEADS, W), value_input.reshape(rows, KEY_HEADS, W)], axis=2
    ).transpose(1, 0, 2)
    qg = jnp.concatenate(
        [query_in.reshape(rows, X, GROUP * W), grad_out.reshape(rows, X, GROUP * W)], axis=2
    ).transpose(1, 0, 2)
    kv = swap(kv)
    kv = kv.reshape(X * rows, 2 * W)
    _, qg = lax.optimization_barrier((add(kv[:16, :W], kv[16:32, :W]), qg))
    qg = swap(qg).reshape(X * rows, 2 * GROUP * W)
    b1, b7 = up(kv), down(kv)
    b2, b6 = up(b1), down(b7)
    b3, b5 = up(b2), down(b6)
    k4, v4 = up(b3[:, :W]), down(b5[:, W:])
    zi = lax.axis_index("z").astype(jnp.int32).reshape(1)
    dq, p0, p1, p2, pk3, pv3, pk4, pv4, pk5, pv5, p6, p7 = attention(
        zi, qg, (kv, b1, b2, b3, k4, v4, b5, b6, b7)
    )
    kd, vu = down(pk4), up(pv4)
    kd = down(jnp.concatenate([add(pk3, kd), pv3], axis=1))
    vu = up(jnp.concatenate([pk5, add(pv5, vu)], axis=1))
    kd, vu = down(add(p2, kd)), up(add(p6, vu))
    kd, vu = down(add(p1, kd)), up(add(p7, vu))
    dkv = (p0.astype(f32) + kd.astype(f32) + vu.astype(f32)).astype(bf16)
    dkv = swap(dkv.reshape(X, rows, 2 * W)).transpose(1, 0, 2)
    dq = swap(dq.reshape(X, rows, GROUP * W)).transpose(1, 0, 2).reshape(rows, HEADS * W)
    dk = dkv[:, :, :W].reshape(rows, KEY_HEADS * W)
    dv = dkv[:, :, W:].reshape(rows, KEY_HEADS * W)
    return dq, dk, dv


def solution(mesh):
    grid = Mesh(mesh.devices.reshape(Z, X, mesh.shape["dp"]), ("z", "x", "dp"))
    spec = P(("dp", "z", "x"), None)
    return jax.shard_map(local, mesh=grid, in_specs=(spec,) * 4, out_specs=(spec,) * 3, check_vma=False)
```

```python
import jax
import jax.numpy as jnp
from jax import lax
from jax.experimental import pallas as pl
from jax.experimental.pallas import tpu as pltpu
from jax.sharding import Mesh, PartitionSpec as P

f32 = jnp.float32
bf16 = jnp.bfloat16
HEADS = 32
KEY_HEADS = 4
GROUP = HEADS // KEY_HEADS
W = 128
X, Z = 4, 8
ORDER = (0, 3, 1, 2)
SCALE = W ** -0.5
EXP2_SCALE = W ** -0.5 * 1.4426950408889634
LIMIT = (80.0 / EXP2_SCALE) ** 2


def nt(a, b):
    return lax.dot_general(a, b, (((1,), (1,)), ((), ())), preferred_element_type=f32)


def nn(a, b):
    return lax.dot_general(a, b, (((1,), (0,)), ((), ())), preferred_element_type=f32)


def attention_kernel(z_ref, qg_ref, b0, b1, b2, b3, k4, v4, b5, b6, b7, dq_ref,
                     o0, o1, o2, o3, ok4, ov4, o5, o6, o7,
                     kr, vr, kt, ps, dps, dka, dva, shift, inv, delta, qn, gn, big):
    R = qg_ref.shape[0]
    T = 2 * R
    h = pl.program_id(0)
    z, x = z_ref[0], z_ref[1]
    blocks = z + 1
    pairs = blocks // 2
    odd = (blocks % 2 == 1) & (pairs >= 1)

    def head(i, base):
        return qg_ref[:, pl.ds(pl.multiple_of(base + i * W, W), W)]

    @pl.when(h == 0)
    def _():
        dka[...] = jnp.zeros_like(dka)
        dva[...] = jnp.zeros_like(dva)
        for r, blk in enumerate((b0, b1, b2, b3, None, b5, b6, b7)):
            kb = k4[...] if blk is None else blk[:, :W]
            vb = v4[...] if blk is None else blk[:, W:]
            kr[r * R:(r + 1) * R, :] = kb
            vr[r * R:(r + 1) * R, :] = vb
            kt[:, r * R:(r + 1) * R] = kb.T
        kk = kr[...].astype(f32)
        kn = jnp.max(nt(jnp.ones((8, W), bf16), (kk * kk).astype(bf16)))
        qq = qg_ref[:, :GROUP * W].astype(f32)
        col = lax.broadcasted_iota(jnp.int32, (GROUP, GROUP * W), 1) // W
        own = lax.broadcasted_iota(jnp.int32, (GROUP, GROUP * W), 0)
        qnorm = jnp.max(nt((col == own).astype(bf16), (qq * qq).astype(bf16)))
        big[0] = kn * qnorm

    def causal(s):
        part = R // X
        kpos = lax.broadcasted_iota(jnp.int32, (part, R), 0)
        qpos = lax.broadcasted_iota(jnp.int32, (part, R), 1)
        return jnp.concatenate(
            [
                jnp.where(kpos + lax.rem(x + o, X) * part <= qpos, s[i * part:(i + 1) * part], -1e30)
                for i, o in enumerate(ORDER)
            ],
            axis=0,
        )

    def forward_begin():
        shift[...] = jnp.zeros_like(shift)

        @pl.when(jnp.logical_not(big[0] <= LIMIT))
        def _():
            q = head(h, 0)

            def peak(r, m):
                s = nt(kr[pl.ds(pl.multiple_of(r * R, R), R), :], q)
                s = jnp.where(r > 0, s, causal(s))
                return jnp.maximum(m, jnp.max(s, axis=0, keepdims=True))

            m = lax.fori_loop(0, blocks, peak, jnp.full((1, R), -1e30, f32))
            shift[...] = jnp.broadcast_to(m * EXP2_SCALE, shift.shape)

    def forward(t, carry, first, n, buf):
        l8, d8 = carry
        q, g = head(h, 0), head(h, GROUP * W)
        m = shift[0:1, :]
        for r in range(n):
            rows = pl.ds(r * R, R) if first else pl.ds(pl.multiple_of(t * T + r * R, R), R)
            s = nt(kr[rows, :], q)
            dp = nt(vr[rows, :], g)
            if first and r == 0:
                s = causal(s)
            elif first:
                s = jnp.where(z >= r, s, -1e30)
            p = jnp.exp2(s * EXP2_SCALE - m)
            ps[buf, rows, :] = p.astype(bf16)
            dps[buf, rows, :] = dp
            l8 = l8 + p.reshape(R // 8, 8, R).sum(0)
            d8 = d8 + (p * dp).reshape(R // 8, 8, R).sum(0)
        return l8, d8

    def forward_end(carry):
        l = jnp.sum(carry[0], axis=0, keepdims=True)
        rl = 1.0 / l
        inv[...] = jnp.broadcast_to(rl, inv.shape)
        delta[...] = jnp.broadcast_to(jnp.sum(carry[1], axis=0, keepdims=True) * rl, delta.shape)
        rc = inv[...].T[:, 0:1]
        qn[...] = (head(h, 0).astype(f32) * rc).astype(bf16)
        gn[...] = (head(h, GROUP * W).astype(f32) * rc).astype(bf16)

    def back(t, dqt, n, buf, q, g, dl):
        for r in range(n):
            rows = pl.ds(pl.multiple_of(t * T + r * R, R), R)
            p = ps[buf, rows, :]
            ds = (p.astype(f32) * (dps[buf, rows, :] - dl)).astype(bf16)
            dva[rows, :] += nn(p, g)
            dka[rows, :] += nn(ds, q)
            dqt = dqt + nn(kt[:, rows], ds)
        return dqt

    zero = (jnp.zeros((8, R), f32), jnp.zeros((8, R), f32))
    zq = jnp.zeros((W, R), f32)

    @pl.when(h == 0)
    def _():
        forward_begin()
        c = forward(0, zero, True, 2, 0)
        c = lax.fori_loop(1, pairs, lambda t, c: forward(t, c, False, 2, 0), c)
        c = lax.cond(odd, lambda c: forward(pairs, c, False, 1, 0), lambda c: c, c)
        forward_end(c)

    @pl.when((h > 0) & (h < GROUP))
    def _():
        new, old = lax.rem(h, 2), lax.rem(h + 1, 2)
        q, g, dl = qn[...], gn[...], delta[0:1, :]
        rl = inv[0:1, :] * SCALE
        forward_begin()

        def both(t, c, first, n):
            f = forward(t, c[:2], first, n, new)
            return f + (back(t, c[2], n, old, q, g, dl),)

        c = both(0, zero + (zq,), True, 2)
        c = lax.fori_loop(1, pairs, lambda t, c: both(t, c, False, 2), c)
        c = lax.cond(odd, lambda c: both(pairs, c, False, 1), lambda c: c, c)
        dq_ref[...] = (c[2] * rl).T.astype(bf16)
        forward_end(c[:2])

    @pl.when(h == GROUP)
    def _():
        old = (GROUP - 1) % 2
        q, g, dl = qn[...], gn[...], delta[0:1, :]
        c = lax.fori_loop(0, jnp.maximum(pairs, 1), lambda t, c: back(t, c, 2, old, q, g, dl), zq)
        c = lax.cond(odd, lambda c: back(pairs, c, 1, old, q, g, dl), lambda c: c, c)
        dq_ref[...] = (c * (inv[0:1, :] * SCALE)).T.astype(bf16)
        for r, out in enumerate((o0, o1, o2, o3, (ok4, ov4), o5, o6, o7)):
            rows = slice(r * R, (r + 1) * R)
            dk = (dka[rows, :] * SCALE).astype(bf16)
            dv = dva[rows, :].astype(bf16)
            if isinstance(out, tuple):
                out[0][...] = dk
                out[1][...] = dv
            else:
                out[:, :W] = dk
                out[:, W:] = dv


def attention(zi, qg, blocks):
    R = qg.shape[0]
    N = Z * R
    wide, half = (R, 2 * W), (R, W)
    outs = [wide] * 4 + [half] * 2 + [wide] * 3

    def whole(shapes):
        return [pl.BlockSpec(memory_space=pltpu.VMEM)] * len(shapes)

    return pl.pallas_call(
        attention_kernel,
        grid_spec=pltpu.PrefetchScalarGridSpec(
            num_scalar_prefetch=1,
            grid=(GROUP + 1,),
            in_specs=whole([qg.shape] + [b.shape for b in blocks]),
            out_specs=[pl.BlockSpec((R, W), lambda h, z: (0, jnp.maximum(h, 1) - 1))] + whole(outs),
            scratch_shapes=[
                pltpu.VMEM((N, W), bf16),
                pltpu.VMEM((N, W), bf16),
                pltpu.VMEM((W, N), bf16),
                pltpu.VMEM((2, N, R), bf16),
                pltpu.VMEM((2, N, R), f32),
                pltpu.VMEM((N, W), f32),
                pltpu.VMEM((N, W), f32),
                pltpu.VMEM((8, R), f32),
                pltpu.VMEM((8, R), f32),
                pltpu.VMEM((8, R), f32),
                pltpu.VMEM((R, W), bf16),
                pltpu.VMEM((R, W), bf16),
                pltpu.SMEM((1,), f32),
            ],
        ),
        out_shape=[jax.ShapeDtypeStruct((R, GROUP * W), bf16)]
        + [jax.ShapeDtypeStruct(s, bf16) for s in outs],
        compiler_params=pltpu.CompilerParams(vmem_limit_bytes=44 * 2**20, dimension_semantics=("arbitrary",)),
    )(zi, qg, *blocks)


def up(v):
    return lax.ppermute(v, "z", [(i, (i + 1) % Z) for i in range(Z)])


def down(v):
    return lax.ppermute(v, "z", [(i, (i - 1) % Z) for i in range(Z)])


def add(a, b):
    return (a.astype(f32) + b.astype(f32)).astype(bf16)


def across(v, d):
    return lax.ppermute(v, "x", [(i, (i + d) % X) for i in range(X)])


def swap(v):
    return lax.all_to_all(v, "x", split_axis=0, concat_axis=0, tiled=True)


def pack_kernel(zx_ref, k_ref, v_ref, *outs):
    for i, out in enumerate(outs):
        col = pl.ds(pl.multiple_of(lax.rem(zx_ref[1] + i, X) * W, W), W)
        out[:, :W] = k_ref[:, col]
        out[:, W:] = v_ref[:, col]


def total_kernel(a_ref, b_ref, c_ref, *outs):
    n = outs[0].shape[0]
    for i, out in enumerate(outs):
        rows = slice(i * n, (i + 1) * n)
        total = a_ref[rows, :].astype(f32) + b_ref[rows, :].astype(f32) + c_ref[rows, :].astype(f32)
        out[...] = total.astype(bf16)


def unpack_kernel(zx_ref, *refs):
    dk_ref, dv_ref = refs[X:]
    for i, piece in enumerate(refs[:X]):
        col = pl.ds(pl.multiple_of(lax.rem(zx_ref[1] + i, X) * W, W), W)
        dk_ref[:, col] = piece[:, :W]
        dv_ref[:, col] = piece[:, W:]


SCALAR = pl.BlockSpec(memory_space=pltpu.SMEM)
ARRAY = pl.BlockSpec(memory_space=pltpu.VMEM)


def local(query_in, key_input, value_input, grad_out):
    rows = query_in.shape[0]
    zx = jnp.stack([lax.axis_index("z"), lax.axis_index("x")]).astype(jnp.int32)
    piece = jax.ShapeDtypeStruct((rows, 2 * W), bf16)
    k0, k1, k2, k3 = pl.pallas_call(
        pack_kernel, in_specs=[SCALAR, ARRAY, ARRAY], out_specs=[ARRAY] * X, out_shape=[piece] * X
    )(zx, key_input, value_input)
    kv = jnp.concatenate([k0, across(k1, 1), across(k3, -1), across(k2, 2)], axis=0)
    _, query_in, grad_out = lax.optimization_barrier((k0, query_in, grad_out))
    qg = jnp.concatenate(
        [query_in.reshape(rows, X, GROUP * W), grad_out.reshape(rows, X, GROUP * W)], axis=2
    ).transpose(1, 0, 2)
    qg = swap(qg).reshape(X * rows, 2 * GROUP * W)
    b1, b7 = up(kv), down(kv)
    b2, b6 = up(b1), down(b7)
    b3, b5 = up(b2), down(b6)
    k4, v4 = up(b3[:, :W]), down(b5[:, W:])
    dq, p0, p1, p2, p3, pk4, pv4, p5, p6, p7 = attention(zx, qg, (kv, b1, b2, b3, k4, v4, b5, b6, b7))
    kd, vu = down(pk4), up(pv4)
    kd = down(add(p3, jnp.pad(kd, ((0, 0), (0, W)))))
    vu = up(add(p5, jnp.pad(vu, ((0, 0), (W, 0)))))
    kd, vu = down(add(p2, kd)), up(add(p6, vu))
    kd, vu = down(add(p1, kd)), up(add(p7, vu))
    f0, f1, f2, f3 = pl.pallas_call(
        total_kernel, in_specs=[ARRAY] * 3, out_specs=[ARRAY] * X, out_shape=[piece] * X
    )(p0, kd, vu)
    heads = jax.ShapeDtypeStruct((rows, KEY_HEADS * W), bf16)
    dk, dv = pl.pallas_call(
        unpack_kernel, in_specs=[SCALAR] + [ARRAY] * X, out_specs=[ARRAY] * 2, out_shape=[heads] * 2
    )(zx, f0, across(f1, -1), across(f3, 2), across(f2, 1))
    dq = swap(dq.reshape(X, rows, GROUP * W)).transpose(1, 0, 2).reshape(rows, HEADS * W)
    return dq, dk, dv


def solution(mesh):
    grid = Mesh(mesh.devices.reshape(Z, X, mesh.shape["dp"]), ("z", "x", "dp"))
    spec = P(("dp", "z", "x"), None)
    return jax.shard_map(local, mesh=grid, in_specs=(spec,) * 4, out_specs=(spec,) * 3, check_vma=False)
```

```python
import jax
import jax.numpy as jnp
from jax import lax
from jax.experimental import pallas as pl
from jax.experimental.pallas import tpu as pltpu
from jax.sharding import Mesh, PartitionSpec as P

f32 = jnp.float32
bf16 = jnp.bfloat16
HEADS = 32
KEY_HEADS = 4
GROUP = HEADS // KEY_HEADS
W = 128
X, Z = 4, 8
SCALE = W ** -0.5
EXP2_SCALE = W ** -0.5 * 1.4426950408889634
LIMIT = (80.0 / EXP2_SCALE) ** 2


def nt(a, b):
    return lax.dot_general(a, b, (((1,), (1,)), ((), ())), preferred_element_type=f32)


def nn(a, b):
    return lax.dot_general(a, b, (((1,), (0,)), ((), ())), preferred_element_type=f32)


def attention_kernel(z_ref, qg_ref, b0, b1, b2, b3, k4, v4, b5, b6, b7, dq_ref,
                     o0, o1, o2, o3, ok4, ov4, o5, o6, o7,
                     kr, vr, kt, ps, dps, dka, dva, shift, inv, delta, qn, gn, big):
    R = qg_ref.shape[0]
    T = 2 * R
    z = z_ref[0]
    blocks = z + 1
    pairs = blocks // 2
    odd = (blocks % 2 == 1) & (pairs >= 1)

    def head(i, base):
        return qg_ref[:, pl.ds(pl.multiple_of(base + i * W, W), W)]

    dka[...] = jnp.zeros_like(dka)
    dva[...] = jnp.zeros_like(dva)
    for r, blk in enumerate((b0, b1, b2, b3, None, b5, b6, b7)):
        kb = k4[...] if blk is None else blk[:, :W]
        vb = v4[...] if blk is None else blk[:, W:]
        kr[r * R:(r + 1) * R, :] = kb
        vr[r * R:(r + 1) * R, :] = vb
        kt[:, r * R:(r + 1) * R] = kb.T
    kk = kr[...].astype(f32)
    kn = jnp.max(nt(jnp.ones((8, W), bf16), (kk * kk).astype(bf16)))
    qq = qg_ref[:, :GROUP * W].astype(f32)
    col = lax.broadcasted_iota(jnp.int32, (GROUP, GROUP * W), 1) // W
    own = lax.broadcasted_iota(jnp.int32, (GROUP, GROUP * W), 0)
    qnorm = jnp.max(nt((col == own).astype(bf16), (qq * qq).astype(bf16)))
    big[0] = kn * qnorm

    def causal(s):
        kpos = lax.broadcasted_iota(jnp.int32, (R, R), 0)
        qpos = lax.broadcasted_iota(jnp.int32, (R, R), 1)
        return jnp.where(kpos <= qpos, s, -1e30)

    def forward_begin(h):
        shift[...] = jnp.zeros_like(shift)

        @pl.when(jnp.logical_not(big[0] <= LIMIT))
        def _():
            q = head(h, 0)

            def peak(r, m):
                s = nt(kr[pl.ds(pl.multiple_of(r * R, R), R), :], q)
                s = jnp.where(r > 0, s, causal(s))
                return jnp.maximum(m, jnp.max(s, axis=0, keepdims=True))

            m = lax.fori_loop(0, blocks, peak, jnp.full((1, R), -1e30, f32))
            shift[...] = jnp.broadcast_to(m * EXP2_SCALE, shift.shape)

    def forward(h, t, carry, first, n, buf):
        l8, d8 = carry
        q, g = head(h, 0), head(h, GROUP * W)
        m = shift[0:1, :]
        for r in range(n):
            rows = pl.ds(r * R, R) if first else pl.ds(pl.multiple_of(t * T + r * R, R), R)
            s = nt(kr[rows, :], q)
            dp = nt(vr[rows, :], g)
            if first and r == 0:
                s = causal(s)
            elif first:
                s = jnp.where(z >= r, s, -1e30)
            p = jnp.exp2(s * EXP2_SCALE - m)
            ps[buf, rows, :] = p.astype(bf16)
            dps[buf, rows, :] = dp
            l8 = l8 + p.reshape(R // 8, 8, R).sum(0)
            d8 = d8 + (p * dp).reshape(R // 8, 8, R).sum(0)
        return l8, d8

    def forward_end(h, carry):
        l = jnp.sum(carry[0], axis=0, keepdims=True)
        rl = 1.0 / l
        inv[...] = jnp.broadcast_to(rl, inv.shape)
        delta[...] = jnp.broadcast_to(jnp.sum(carry[1], axis=0, keepdims=True) * rl, delta.shape)
        rc = inv[...].T[:, 0:1]
        qn[...] = (head(h, 0).astype(f32) * rc).astype(bf16)
        gn[...] = (head(h, GROUP * W).astype(f32) * rc).astype(bf16)

    def back(t, dqt, n, buf, q, g, dl):
        for r in range(n):
            rows = pl.ds(pl.multiple_of(t * T + r * R, R), R)
            p = ps[buf, rows, :]
            ds = (p.astype(f32) * (dps[buf, rows, :] - dl)).astype(bf16)
            dva[rows, :] += nn(p, g)
            dka[rows, :] += nn(ds, q)
            dqt = dqt + nn(kt[:, rows], ds)
        return dqt

    zero = (jnp.zeros((8, R), f32), jnp.zeros((8, R), f32))
    zq = jnp.zeros((W, R), f32)

    def store(h, dqt, rl):
        dq_ref[:, pl.ds(pl.multiple_of(h * W, W), W)] = (dqt * rl).T.astype(bf16)

    def first_head():
        forward_begin(0)
        c = forward(0, 0, zero, True, 2, 0)
        c = lax.fori_loop(1, pairs, lambda t, c: forward(0, t, c, False, 2, 0), c)
        c = lax.cond(odd, lambda c: forward(0, pairs, c, False, 1, 0), lambda c: c, c)
        forward_end(0, c)

    def next_head(h, _):
        new, old = lax.rem(h, 2), lax.rem(h + 1, 2)
        q, g, dl = qn[...], gn[...], delta[0:1, :]
        rl = inv[0:1, :] * SCALE
        forward_begin(h)

        def both(t, c, first, n):
            f = forward(h, t, c[:2], first, n, new)
            return f + (back(t, c[2], n, old, q, g, dl),)

        c = both(0, zero + (zq,), True, 2)
        c = lax.fori_loop(1, pairs, lambda t, c: both(t, c, False, 2), c)
        c = lax.cond(odd, lambda c: both(pairs, c, False, 1), lambda c: c, c)
        store(h - 1, c[2], rl)
        forward_end(h, c[:2])
        return 0

    def last_head():
        old = (GROUP - 1) % 2
        q, g, dl = qn[...], gn[...], delta[0:1, :]
        c = lax.fori_loop(0, jnp.maximum(pairs, 1), lambda t, c: back(t, c, 2, old, q, g, dl), zq)
        c = lax.cond(odd, lambda c: back(pairs, c, 1, old, q, g, dl), lambda c: c, c)
        store(GROUP - 1, c, inv[0:1, :] * SCALE)

    first_head()
    lax.fori_loop(1, GROUP, next_head, 0)
    last_head()
    for r, out in enumerate((o0, o1, o2, o3, (ok4, ov4), o5, o6, o7)):
        rows = slice(r * R, (r + 1) * R)
        dk = (dka[rows, :] * SCALE).astype(bf16)
        dv = dva[rows, :].astype(bf16)
        if isinstance(out, tuple):
            out[0][...] = dk
            out[1][...] = dv
        else:
            out[:, :W] = dk
            out[:, W:] = dv


def attention(zi, qg, blocks):
    R = qg.shape[0]
    N = Z * R
    wide, half = (R, 2 * W), (R, W)
    outs = [wide] * 4 + [half] * 2 + [wide] * 3

    def whole(shapes):
        return [pl.BlockSpec(s, lambda i, zx: (0, 0)) for s in shapes]

    return pl.pallas_call(
        attention_kernel,
        grid_spec=pltpu.PrefetchScalarGridSpec(
            num_scalar_prefetch=1,
            grid=(1,),
            in_specs=whole([qg.shape] + [b.shape for b in blocks]),
            out_specs=whole([(R, GROUP * W)] + outs),
            scratch_shapes=[
                pltpu.VMEM((N, W), bf16),
                pltpu.VMEM((N, W), bf16),
                pltpu.VMEM((W, N), bf16),
                pltpu.VMEM((2, N, R), bf16),
                pltpu.VMEM((2, N, R), f32),
                pltpu.VMEM((N, W), f32),
                pltpu.VMEM((N, W), f32),
                pltpu.VMEM((8, R), f32),
                pltpu.VMEM((8, R), f32),
                pltpu.VMEM((8, R), f32),
                pltpu.VMEM((R, W), bf16),
                pltpu.VMEM((R, W), bf16),
                pltpu.SMEM((1,), f32),
            ],
        ),
        out_shape=[jax.ShapeDtypeStruct((R, GROUP * W), bf16)]
        + [jax.ShapeDtypeStruct(s, bf16) for s in outs],
        compiler_params=pltpu.CompilerParams(vmem_limit_bytes=60 * 2**20, dimension_semantics=("arbitrary",)),
    )(zi, qg, *blocks)


def up(v):
    return lax.ppermute(v, "z", [(i, (i + 1) % Z) for i in range(Z)])


def down(v):
    return lax.ppermute(v, "z", [(i, (i - 1) % Z) for i in range(Z)])


def add(a, b):
    return (a.astype(f32) + b.astype(f32)).astype(bf16)


def across(v, d):
    return lax.ppermute(v, "x", [(i, (i + d) % X) for i in range(X)])


def swap(v):
    return lax.all_to_all(v, "x", split_axis=0, concat_axis=0, tiled=True)


def pack_kernel(zx_ref, k_ref, v_ref, *outs):
    for i, out in enumerate(outs):
        col = pl.ds(pl.multiple_of(lax.rem(zx_ref[1] + i, X) * W, W), W)
        out[:, :W] = k_ref[:, col]
        out[:, W:] = v_ref[:, col]


def total_kernel(zx_ref, a_ref, b_ref, c_ref, *outs):
    n = outs[0].shape[0]
    for i, out in enumerate(outs):
        rows = pl.ds(pl.multiple_of(lax.rem(zx_ref[1] + i, X) * n, n), n)
        total = a_ref[rows, :].astype(f32) + b_ref[rows, :].astype(f32) + c_ref[rows, :].astype(f32)
        out[...] = total.astype(bf16)


def unpack_kernel(zx_ref, *refs):
    dk_ref, dv_ref = refs[X:]
    for i, piece in enumerate(refs[:X]):
        col = pl.ds(pl.multiple_of(lax.rem(zx_ref[1] + i, X) * W, W), W)
        dk_ref[:, col] = piece[:, :W]
        dv_ref[:, col] = piece[:, W:]


SCALAR = pl.BlockSpec(memory_space=pltpu.SMEM)
ARRAY = pl.BlockSpec(memory_space=pltpu.VMEM)


def local(query_in, key_input, value_input, grad_out):
    rows = query_in.shape[0]
    zx = jnp.stack([lax.axis_index("z"), lax.axis_index("x")]).astype(jnp.int32)
    piece = jax.ShapeDtypeStruct((rows, 2 * W), bf16)
    k0, k1, k2, k3 = pl.pallas_call(
        pack_kernel, in_specs=[SCALAR, ARRAY, ARRAY], out_specs=[ARRAY] * X, out_shape=[piece] * X
    )(zx, key_input, value_input)
    kv = jnp.zeros((X * rows, 2 * W), bf16)
    for d, part in ((0, k0), (1, across(k1, 1)), (3, across(k3, -1)), (2, across(k2, 2))):
        kv = lax.dynamic_update_slice(kv, part, (lax.rem(zx[1] + X - d, X) * rows, 0))
    qg = jnp.concatenate(
        [query_in.reshape(rows, X, GROUP * W), grad_out.reshape(rows, X, GROUP * W)], axis=2
    ).transpose(1, 0, 2)
    kv, qg = lax.optimization_barrier((kv, qg))
    qg = swap(qg).reshape(X * rows, 2 * GROUP * W)
    b1, b7 = up(kv), down(kv)
    b2, b6 = up(b1), down(b7)
    b3, b5 = up(b2), down(b6)
    k4, v4 = up(b3[:, :W]), down(b5[:, W:])
    dq, p0, p1, p2, p3, pk4, pv4, p5, p6, p7 = attention(zx, qg, (kv, b1, b2, b3, k4, v4, b5, b6, b7))
    kd, vu = down(pk4), up(pv4)
    kd = down(add(p3, jnp.pad(kd, ((0, 0), (0, W)))))
    vu = up(add(p5, jnp.pad(vu, ((0, 0), (W, 0)))))
    kd, vu = down(add(p2, kd)), up(add(p6, vu))
    kd, vu = down(add(p1, kd)), up(add(p7, vu))
    f0, f1, f2, f3 = pl.pallas_call(
        total_kernel, in_specs=[SCALAR] + [ARRAY] * 3, out_specs=[ARRAY] * X, out_shape=[piece] * X
    )(zx, p0, kd, vu)
    heads = jax.ShapeDtypeStruct((rows, KEY_HEADS * W), bf16)
    dk, dv = pl.pallas_call(
        unpack_kernel, in_specs=[SCALAR] + [ARRAY] * X, out_specs=[ARRAY] * 2, out_shape=[heads] * 2
    )(zx, f0, across(f3, -1), across(f2, 2), across(f1, 1))
    dq = swap(dq.reshape(X, rows, GROUP * W)).transpose(1, 0, 2).reshape(rows, HEADS * W)
    return dq, dk, dv


def solution(mesh):
    grid = Mesh(mesh.devices.reshape(Z, X, mesh.shape["dp"]), ("z", "x", "dp"))
    spec = P(("dp", "z", "x"), None)
    return jax.shard_map(local, mesh=grid, in_specs=(spec,) * 4, out_specs=(spec,) * 3, check_vma=False)
```

```python
import jax
import jax.numpy as jnp
from jax import lax
from jax.experimental import pallas as pl
from jax.experimental.pallas import tpu as pltpu
from jax.sharding import Mesh, PartitionSpec as P

f32 = jnp.float32
bf16 = jnp.bfloat16
HEADS = 32
KEY_HEADS = 4
GROUP = HEADS // KEY_HEADS
W = 128
X, Z = 4, 8
GANG = 8
SCALE = W ** -0.5
EXP2_SCALE = W ** -0.5 * 1.4426950408889634
LIMIT = (80.0 / EXP2_SCALE) ** 2


def nt(a, b):
    return lax.dot_general(a, b, (((1,), (1,)), ((), ())), preferred_element_type=f32)


def nn(a, b):
    return lax.dot_general(a, b, (((1,), (0,)), ((), ())), preferred_element_type=f32)


def attention_kernel(z_ref, qg_ref, b0, b1, b2, b3, k4, v4, b5, b6, b7, dq_ref,
                     o0, o1, o2, o3, ok4, ov4, o5, o6, o7,
                     kr, vr, kt, ps, dps, dka, dva, shift, inv, delta, qn, gn, big):
    R = qg_ref.shape[0]
    z = z_ref[0]
    blocks = z + 1

    def head(i, base):
        return qg_ref[:, pl.ds(pl.multiple_of(base + i * W, W), W)]

    dka[...] = jnp.zeros_like(dka)
    dva[...] = jnp.zeros_like(dva)
    for r, blk in enumerate((b0, b1, b2, b3, None, b5, b6, b7)):
        kb = k4[...] if blk is None else blk[:, :W]
        vb = v4[...] if blk is None else blk[:, W:]
        kr[r * R:(r + 1) * R, :] = kb
        vr[r * R:(r + 1) * R, :] = vb
        kt[:, r * R:(r + 1) * R] = kb.T
    kk = kr[...].astype(f32)
    kn = jnp.max(nt(jnp.ones((8, W), bf16), (kk * kk).astype(bf16)))
    qq = qg_ref[:, :GROUP * W].astype(f32)
    col = lax.broadcasted_iota(jnp.int32, (GROUP, GROUP * W), 1) // W
    own = lax.broadcasted_iota(jnp.int32, (GROUP, GROUP * W), 0)
    qnorm = jnp.max(nt((col == own).astype(bf16), (qq * qq).astype(bf16)))
    big[0] = kn * qnorm

    def causal(s):
        kpos = lax.broadcasted_iota(jnp.int32, (R, R), 0)
        qpos = lax.broadcasted_iota(jnp.int32, (R, R), 1)
        return jnp.where(kpos <= qpos, s, -1e30)

    def forward_begin(h):
        shift[...] = jnp.zeros_like(shift)

        @pl.when(jnp.logical_not(big[0] <= LIMIT))
        def _():
            q = head(h, 0)

            def peak(r, m):
                s = nt(kr[pl.ds(pl.multiple_of(r * R, R), R), :], q)
                s = jnp.where(r > 0, s, causal(s))
                return jnp.maximum(m, jnp.max(s, axis=0, keepdims=True))

            m = lax.fori_loop(0, blocks, peak, jnp.full((1, R), -1e30, f32))
            shift[...] = jnp.broadcast_to(m * EXP2_SCALE, shift.shape)

    def forward(h, r0, carry, buf):
        l8, d8 = carry
        q, g = head(h, 0), head(h, GROUP * W)
        for r in range(r0, r0 + GANG):
            rows = slice(r * R, (r + 1) * R)
            s = nt(kr[rows, :], q)
            dp = nt(vr[rows, :], g)
            m = shift[0:1, :]
            if r == 0:
                s = causal(s)
            else:
                m = m + jnp.where(z >= r, 0.0, 1e30)
            p = jnp.exp2(s * EXP2_SCALE - m)
            ps[buf, rows, :] = p.astype(bf16)
            dps[buf, rows, :] = dp
            l8 = l8 + p.reshape(R // 8, 8, R).sum(0)
            d8 = d8 + (p * dp).reshape(R // 8, 8, R).sum(0)
        return l8, d8

    def forward_end(h, carry):
        l = jnp.sum(carry[0], axis=0, keepdims=True)
        rl = 1.0 / l
        inv[...] = jnp.broadcast_to(rl, inv.shape)
        delta[...] = jnp.broadcast_to(jnp.sum(carry[1], axis=0, keepdims=True) * rl, delta.shape)
        rc = inv[...].T[:, 0:1]
        qn[...] = (head(h, 0).astype(f32) * rc).astype(bf16)
        gn[...] = (head(h, GROUP * W).astype(f32) * rc).astype(bf16)

    def back(r0, dqt, buf, q, g, dl):
        for r in range(r0, r0 + GANG):
            rows = slice(r * R, (r + 1) * R)
            p = ps[buf, rows, :]
            ds = (p.astype(f32) * (dps[buf, rows, :] - dl)).astype(bf16)
            dva[rows, :] += nn(p, g)
            dka[rows, :] += nn(ds, q)
            dqt = dqt + nn(kt[:, rows], ds)
        return dqt

    def gangs(step, carry):
        carry = step(0, carry)
        for r0 in range(GANG, Z, GANG):
            carry = lax.cond(z >= r0, lambda c: step(r0, c), lambda c: c, carry)
        return carry

    zero = (jnp.zeros((8, R), f32), jnp.zeros((8, R), f32))
    zq = jnp.zeros((W, R), f32)

    def store(h, dqt, rl):
        dq_ref[:, pl.ds(pl.multiple_of(h * W, W), W)] = (dqt * rl).T.astype(bf16)

    def first_head():
        forward_begin(0)
        forward_end(0, gangs(lambda r0, c: forward(0, r0, c, 0), zero))

    def next_head(h, _):
        new, old = lax.rem(h, 2), lax.rem(h + 1, 2)
        q, g, dl = qn[...], gn[...], delta[0:1, :]
        rl = inv[0:1, :] * SCALE
        forward_begin(h)

        def both(r0, c):
            return forward(h, r0, c[:2], new) + (back(r0, c[2], old, q, g, dl),)

        c = gangs(both, zero + (zq,))
        store(h - 1, c[2], rl)
        forward_end(h, c[:2])
        return 0

    def last_head():
        q, g, dl = qn[...], gn[...], delta[0:1, :]
        dqt = gangs(lambda r0, c: back(r0, c, (GROUP - 1) % 2, q, g, dl), zq)
        store(GROUP - 1, dqt, inv[0:1, :] * SCALE)

    first_head()
    lax.fori_loop(1, GROUP, next_head, 0)
    last_head()
    for r, out in enumerate((o0, o1, o2, o3, (ok4, ov4), o5, o6, o7)):
        rows = slice(r * R, (r + 1) * R)
        dk = (dka[rows, :] * SCALE).astype(bf16)
        dv = dva[rows, :].astype(bf16)
        if isinstance(out, tuple):
            out[0][...] = dk
            out[1][...] = dv
        else:
            out[:, :W] = dk
            out[:, W:] = dv


def attention(zi, qg, blocks):
    R = qg.shape[0]
    N = Z * R
    wide, half = (R, 2 * W), (R, W)
    outs = [wide] * 4 + [half] * 2 + [wide] * 3

    def whole(shapes):
        return [pl.BlockSpec(s, lambda i, zx: (0, 0)) for s in shapes]

    return pl.pallas_call(
        attention_kernel,
        grid_spec=pltpu.PrefetchScalarGridSpec(
            num_scalar_prefetch=1,
            grid=(1,),
            in_specs=whole([qg.shape] + [b.shape for b in blocks]),
            out_specs=whole([(R, GROUP * W)] + outs),
            scratch_shapes=[
                pltpu.VMEM((N, W), bf16),
                pltpu.VMEM((N, W), bf16),
                pltpu.VMEM((W, N), bf16),
                pltpu.VMEM((2, N, R), bf16),
                pltpu.VMEM((2, N, R), f32),
                pltpu.VMEM((N, W), f32),
                pltpu.VMEM((N, W), f32),
                pltpu.VMEM((8, R), f32),
                pltpu.VMEM((8, R), f32),
                pltpu.VMEM((8, R), f32),
                pltpu.VMEM((R, W), bf16),
                pltpu.VMEM((R, W), bf16),
                pltpu.SMEM((1,), f32),
            ],
        ),
        out_shape=[jax.ShapeDtypeStruct((R, GROUP * W), bf16)]
        + [jax.ShapeDtypeStruct(s, bf16) for s in outs],
        compiler_params=pltpu.CompilerParams(vmem_limit_bytes=60 * 2**20, dimension_semantics=("arbitrary",)),
    )(zi, qg, *blocks)


def up(v):
    return lax.ppermute(v, "z", [(i, (i + 1) % Z) for i in range(Z)])


def down(v):
    return lax.ppermute(v, "z", [(i, (i - 1) % Z) for i in range(Z)])


def add(a, b):
    return (a.astype(f32) + b.astype(f32)).astype(bf16)


def across(v, d):
    return lax.ppermute(v, "x", [(i, (i + d) % X) for i in range(X)])


def swap(v):
    return lax.all_to_all(v, "x", split_axis=0, concat_axis=0, tiled=True)


def pack_kernel(zx_ref, k_ref, v_ref, *outs):
    for i, out in enumerate(outs):
        col = pl.ds(pl.multiple_of(lax.rem(zx_ref[1] + i, X) * W, W), W)
        out[:, :W] = k_ref[:, col]
        out[:, W:] = v_ref[:, col]


def total_kernel(zx_ref, a_ref, b_ref, c_ref, *outs):
    n = outs[0].shape[0]
    for i, out in enumerate(outs):
        rows = pl.ds(pl.multiple_of(lax.rem(zx_ref[1] + i, X) * n, n), n)
        total = a_ref[rows, :].astype(f32) + b_ref[rows, :].astype(f32) + c_ref[rows, :].astype(f32)
        out[...] = total.astype(bf16)


def unpack_kernel(zx_ref, *refs):
    dk_ref, dv_ref = refs[X:]
    for i, piece in enumerate(refs[:X]):
        col = pl.ds(pl.multiple_of(lax.rem(zx_ref[1] + i, X) * W, W), W)
        dk_ref[:, col] = piece[:, :W]
        dv_ref[:, col] = piece[:, W:]


SCALAR = pl.BlockSpec(memory_space=pltpu.SMEM)
ARRAY = pl.BlockSpec(memory_space=pltpu.VMEM)


def local(query_in, key_input, value_input, grad_out):
    rows = query_in.shape[0]
    zx = jnp.stack([lax.axis_index("z"), lax.axis_index("x")]).astype(jnp.int32)
    piece = jax.ShapeDtypeStruct((rows, 2 * W), bf16)
    k0, k1, k2, k3 = pl.pallas_call(
        pack_kernel, in_specs=[SCALAR, ARRAY, ARRAY], out_specs=[ARRAY] * X, out_shape=[piece] * X
    )(zx, key_input, value_input)
    kv = jnp.zeros((X * rows, 2 * W), bf16)
    for d, part in ((0, k0), (1, across(k1, 1)), (3, across(k3, -1)), (2, across(k2, 2))):
        kv = lax.dynamic_update_slice(kv, part, (lax.rem(zx[1] + X - d, X) * rows, 0))
    qg = jnp.concatenate(
        [query_in.reshape(rows, X, GROUP * W), grad_out.reshape(rows, X, GROUP * W)], axis=2
    ).transpose(1, 0, 2)
    kv, qg = lax.optimization_barrier((kv, qg))
    qg = swap(qg).reshape(X * rows, 2 * GROUP * W)
    b1, b7 = up(kv), down(kv)
    b2, b6 = up(b1), down(b7)
    b3, b5 = up(b2), down(b6)
    k4, v4 = up(b3[:, :W]), down(b5[:, W:])
    dq, p0, p1, p2, p3, pk4, pv4, p5, p6, p7 = attention(zx, qg, (kv, b1, b2, b3, k4, v4, b5, b6, b7))
    kd, vu = down(pk4), up(pv4)
    kd = down(add(p3, jnp.pad(kd, ((0, 0), (0, W)))))
    vu = up(add(p5, jnp.pad(vu, ((0, 0), (W, 0)))))
    kd, vu = down(add(p2, kd)), up(add(p6, vu))
    kd, vu = down(add(p1, kd)), up(add(p7, vu))
    f0, f1, f2, f3 = pl.pallas_call(
        total_kernel, in_specs=[SCALAR] + [ARRAY] * 3, out_specs=[ARRAY] * X, out_shape=[piece] * X
    )(zx, p0, kd, vu)
    heads = jax.ShapeDtypeStruct((rows, KEY_HEADS * W), bf16)
    dk, dv = pl.pallas_call(
        unpack_kernel, in_specs=[SCALAR] + [ARRAY] * X, out_specs=[ARRAY] * 2, out_shape=[heads] * 2
    )(zx, f0, across(f3, -1), across(f2, 2), across(f1, 1))
    dq = swap(dq.reshape(X, rows, GROUP * W)).transpose(1, 0, 2).reshape(rows, HEADS * W)
    return dq, dk, dv


def solution(mesh):
    grid = Mesh(mesh.devices.reshape(Z, X, mesh.shape["dp"]), ("z", "x", "dp"))
    spec = P(("dp", "z", "x"), None)
    return jax.shard_map(local, mesh=grid, in_specs=(spec,) * 4, out_specs=(spec,) * 3, check_vma=False)
```

```python
import jax
import jax.numpy as jnp
from jax import lax
from jax.experimental import pallas as pl
from jax.experimental.pallas import tpu as pltpu
from jax.sharding import Mesh, PartitionSpec as P

f32 = jnp.float32
bf16 = jnp.bfloat16
HEADS = 32
KEY_HEADS = 4
GROUP = HEADS // KEY_HEADS
W = 128
X, Z = 4, 8
GANG = 8
SCALE = W ** -0.5
EXP2_SCALE = W ** -0.5 * 1.4426950408889634
LIMIT = (80.0 / EXP2_SCALE) ** 2


def nt(a, b):
    return lax.dot_general(a, b, (((1,), (1,)), ((), ())), preferred_element_type=f32)


def nn(a, b):
    return lax.dot_general(a, b, (((1,), (0,)), ((), ())), preferred_element_type=f32)


def attention_kernel(z_ref, qg_ref, b0, b1, b2, b3, k4, v4, b5, b6, b7, dq_ref,
                     o0, o1, o2, o3, ok4, ov4, o5, o6, o7,
                     kr, vr, kt, ps, dps, dka, dva, shift, inv, delta, qn, gn, big):
    R = qg_ref.shape[0]
    z = z_ref[0]
    blocks = z + 1

    def head(i, base):
        return qg_ref[:, pl.ds(pl.multiple_of(base + i * W, W), W)]

    dka[...] = jnp.zeros_like(dka)
    dva[...] = jnp.zeros_like(dva)
    for r, blk in enumerate((b0, b1, b2, b3, None, b5, b6, b7)):
        kb = k4[...] if blk is None else blk[:, :W]
        vb = v4[...] if blk is None else blk[:, W:]
        kr[r * R:(r + 1) * R, :] = kb
        vr[r * R:(r + 1) * R, :] = vb
        kt[:, r * R:(r + 1) * R] = kb.T
    kk = kr[...].astype(f32)
    kn = jnp.max(nt(jnp.ones((8, W), bf16), (kk * kk).astype(bf16)))
    qq = qg_ref[:, :GROUP * W].astype(f32)
    col = lax.broadcasted_iota(jnp.int32, (GROUP, GROUP * W), 1) // W
    own = lax.broadcasted_iota(jnp.int32, (GROUP, GROUP * W), 0)
    qnorm = jnp.max(nt((col == own).astype(bf16), (qq * qq).astype(bf16)))
    big[0] = kn * qnorm

    def causal(s):
        kpos = lax.broadcasted_iota(jnp.int32, (R, R), 0)
        qpos = lax.broadcasted_iota(jnp.int32, (R, R), 1)
        return jnp.where(kpos <= qpos, s, -1e30)

    def forward_begin(h):
        shift[...] = jnp.zeros_like(shift)

        @pl.when(jnp.logical_not(big[0] <= LIMIT))
        def _():
            q = head(h, 0)

            def peak(r, m):
                s = nt(kr[pl.ds(pl.multiple_of(r * R, R), R), :], q)
                s = jnp.where(r > 0, s, causal(s))
                return jnp.maximum(m, jnp.max(s, axis=0, keepdims=True))

            m = lax.fori_loop(0, blocks, peak, jnp.full((1, R), -1e30, f32))
            shift[...] = jnp.broadcast_to(m * EXP2_SCALE, shift.shape)

    def forward(h, r0, carry, buf):
        l8, d8 = carry
        q, g = head(h, 0), head(h, GROUP * W)
        for r in range(r0, r0 + GANG):
            rows = slice(r * R, (r + 1) * R)
            s = nt(kr[rows, :], q)
            dp = nt(vr[rows, :], g)
            m = shift[0:1, :]
            if r == 0:
                s = causal(s)
            else:
                m = m + jnp.where(z >= r, 0.0, 1e30)
            p = jnp.exp2(s * EXP2_SCALE - m)
            ps[buf, rows, :] = p.astype(bf16)
            dps[buf, rows, :] = dp
            l8 = l8 + p.reshape(R // 8, 8, R).sum(0)
            d8 = d8 + (p * dp).reshape(R // 8, 8, R).sum(0)
        return l8, d8

    def forward_end(h, carry):
        l = jnp.sum(carry[0], axis=0, keepdims=True)
        rl = 1.0 / l
        inv[...] = jnp.broadcast_to(rl, inv.shape)
        delta[...] = jnp.broadcast_to(jnp.sum(carry[1], axis=0, keepdims=True) * rl, delta.shape)
        rc = inv[...].T[:, 0:1]
        qn[...] = (head(h, 0).astype(f32) * rc).astype(bf16)
        gn[...] = (head(h, GROUP * W).astype(f32) * rc).astype(bf16)

    def back(r0, dqt, buf, q, g, dl):
        for r in range(r0, r0 + GANG):
            rows = slice(r * R, (r + 1) * R)
            p = ps[buf, rows, :]
            ds = (p.astype(f32) * (dps[buf, rows, :] - dl)).astype(bf16)
            dva[rows, :] += nn(p, g)
            dka[rows, :] += nn(ds, q)
            dqt = dqt + nn(kt[:, rows], ds)
        return dqt

    def gangs(step, carry):
        carry = step(0, carry)
        for r0 in range(GANG, Z, GANG):
            carry = lax.cond(z >= r0, lambda c: step(r0, c), lambda c: c, carry)
        return carry

    zero = (jnp.zeros((8, R), f32), jnp.zeros((8, R), f32))
    zq = jnp.zeros((W, R), f32)

    def store(h, dqt, rl):
        dq_ref[:, pl.ds(pl.multiple_of(h * W, W), W)] = (dqt * rl).T.astype(bf16)

    def first_head():
        forward_begin(0)
        forward_end(0, gangs(lambda r0, c: forward(0, r0, c, 0), zero))

    def next_head(h, _):
        new, old = lax.rem(h, 2), lax.rem(h + 1, 2)
        q, g, dl = qn[...], gn[...], delta[0:1, :]
        rl = inv[0:1, :] * SCALE
        forward_begin(h)

        def both(r0, c):
            dqt = back(r0, c[2], old, q, g, dl)
            return forward(h, r0, c[:2], new) + (dqt,)

        c = gangs(both, zero + (zq,))
        store(h - 1, c[2], rl)
        forward_end(h, c[:2])
        return 0

    def last_head():
        q, g, dl = qn[...], gn[...], delta[0:1, :]
        dqt = gangs(lambda r0, c: back(r0, c, (GROUP - 1) % 2, q, g, dl), zq)
        store(GROUP - 1, dqt, inv[0:1, :] * SCALE)

    first_head()
    lax.fori_loop(1, GROUP, next_head, 0)
    last_head()
    for r, out in enumerate((o0, o1, o2, o3, (ok4, ov4), o5, o6, o7)):
        rows = slice(r * R, (r + 1) * R)
        dk = (dka[rows, :] * SCALE).astype(bf16)
        dv = dva[rows, :].astype(bf16)
        if isinstance(out, tuple):
            out[0][...] = dk
            out[1][...] = dv
        else:
            out[:, :W] = dk
            out[:, W:] = dv


def attention(zi, qg, blocks):
    R = qg.shape[0]
    N = Z * R
    wide, half = (R, 2 * W), (R, W)
    outs = [wide] * 4 + [half] * 2 + [wide] * 3

    def whole(shapes):
        return [pl.BlockSpec(s, lambda i, zx: (0, 0)) for s in shapes]

    return pl.pallas_call(
        attention_kernel,
        grid_spec=pltpu.PrefetchScalarGridSpec(
            num_scalar_prefetch=1,
            grid=(1,),
            in_specs=whole([qg.shape] + [b.shape for b in blocks]),
            out_specs=whole([(R, GROUP * W)]) + [pl.BlockSpec(memory_space=pltpu.VMEM)] * len(outs),
            scratch_shapes=[
                pltpu.VMEM((N, W), bf16),
                pltpu.VMEM((N, W), bf16),
                pltpu.VMEM((W, N), bf16),
                pltpu.VMEM((2, N, R), bf16),
                pltpu.VMEM((2, N, R), f32),
                pltpu.VMEM((N, W), f32),
                pltpu.VMEM((N, W), f32),
                pltpu.VMEM((8, R), f32),
                pltpu.VMEM((8, R), f32),
                pltpu.VMEM((8, R), f32),
                pltpu.VMEM((R, W), bf16),
                pltpu.VMEM((R, W), bf16),
                pltpu.SMEM((1,), f32),
            ],
        ),
        out_shape=[jax.ShapeDtypeStruct((R, GROUP * W), bf16)]
        + [jax.ShapeDtypeStruct(s, bf16) for s in outs],
        compiler_params=pltpu.CompilerParams(vmem_limit_bytes=48 * 2**20, dimension_semantics=("arbitrary",)),
    )(zi, qg, *blocks)


def up(v):
    return lax.ppermute(v, "z", [(i, (i + 1) % Z) for i in range(Z)])


def down(v):
    return lax.ppermute(v, "z", [(i, (i - 1) % Z) for i in range(Z)])


def add(a, b):
    return (a.astype(f32) + b.astype(f32)).astype(bf16)


def across(v, d):
    return lax.ppermute(v, "x", [(i, (i + d) % X) for i in range(X)])


def swap(v):
    return lax.all_to_all(v, "x", split_axis=0, concat_axis=0, tiled=True)


def pack_kernel(zx_ref, k_ref, v_ref, *outs):
    for i, out in enumerate(outs):
        col = pl.ds(pl.multiple_of(lax.rem(zx_ref[1] + i, X) * W, W), W)
        out[:, :W] = k_ref[:, col]
        out[:, W:] = v_ref[:, col]


def total_kernel(zx_ref, a_ref, b_ref, c_ref, *outs):
    n = outs[0].shape[0]
    for i, out in enumerate(outs):
        rows = pl.ds(pl.multiple_of(lax.rem(zx_ref[1] + i, X) * n, n), n)
        total = a_ref[rows, :].astype(f32) + b_ref[rows, :].astype(f32) + c_ref[rows, :].astype(f32)
        out[...] = total.astype(bf16)


def unpack_kernel(zx_ref, *refs):
    dk_ref, dv_ref = refs[X:]
    for i, piece in enumerate(refs[:X]):
        col = pl.ds(pl.multiple_of(lax.rem(zx_ref[1] + i, X) * W, W), W)
        dk_ref[:, col] = piece[:, :W]
        dv_ref[:, col] = piece[:, W:]


SCALAR = pl.BlockSpec(memory_space=pltpu.SMEM)
ARRAY = pl.BlockSpec(memory_space=pltpu.VMEM)


def local(query_in, key_input, value_input, grad_out):
    rows = query_in.shape[0]
    zx = jnp.stack([lax.axis_index("z"), lax.axis_index("x")]).astype(jnp.int32)
    piece = jax.ShapeDtypeStruct((rows, 2 * W), bf16)
    k0, k1, k2, k3 = pl.pallas_call(
        pack_kernel, in_specs=[SCALAR, ARRAY, ARRAY], out_specs=[ARRAY] * X, out_shape=[piece] * X
    )(zx, key_input, value_input)
    kv = jnp.zeros((X * rows, 2 * W), bf16)
    for d, part in ((0, k0), (1, across(k1, 1)), (3, across(k3, -1)), (2, across(k2, 2))):
        kv = lax.dynamic_update_slice(kv, part, (lax.rem(zx[1] + X - d, X) * rows, 0))
    qg = jnp.concatenate(
        [query_in.reshape(rows, X, GROUP * W), grad_out.reshape(rows, X, GROUP * W)], axis=2
    ).transpose(1, 0, 2)
    kv, qg = lax.optimization_barrier((kv, qg))
    qg = swap(qg).reshape(X * rows, 2 * GROUP * W)
    b1, b7 = up(kv), down(kv)
    b2, b6 = up(b1), down(b7)
    b3, b5 = up(b2), down(b6)
    k4, v4 = up(b3[:, :W]), down(b5[:, W:])
    dq, p0, p1, p2, p3, pk4, pv4, p5, p6, p7 = attention(zx, qg, (kv, b1, b2, b3, k4, v4, b5, b6, b7))
    kd, vu = down(pk4), up(pv4)
    kd = down(add(p3, jnp.pad(kd, ((0, 0), (0, W)))))
    vu = up(add(p5, jnp.pad(vu, ((0, 0), (W, 0)))))
    kd, vu = down(add(p2, kd)), up(add(p6, vu))
    kd, vu = down(add(p1, kd)), up(add(p7, vu))
    f0, f1, f2, f3 = pl.pallas_call(
        total_kernel, in_specs=[SCALAR] + [ARRAY] * 3, out_specs=[ARRAY] * X, out_shape=[piece] * X
    )(zx, p0, kd, vu)
    heads = jax.ShapeDtypeStruct((rows, KEY_HEADS * W), bf16)
    dk, dv = pl.pallas_call(
        unpack_kernel, in_specs=[SCALAR] + [ARRAY] * X, out_specs=[ARRAY] * 2, out_shape=[heads] * 2
    )(zx, f0, across(f3, -1), across(f2, 2), across(f1, 1))
    dq = swap(dq.reshape(X, rows, GROUP * W)).transpose(1, 0, 2).reshape(rows, HEADS * W)
    return dq, dk, dv


def solution(mesh):
    grid = Mesh(mesh.devices.reshape(Z, X, mesh.shape["dp"]), ("z", "x", "dp"))
    spec = P(("dp", "z", "x"), None)
    return jax.shard_map(local, mesh=grid, in_specs=(spec,) * 4, out_specs=(spec,) * 3, check_vma=False)
```
